32 devices in a mesh: cfg: 2 (over x), ta: 2 (over core), sa: 8 (over z, y).
Axes of the slice: x: 2, y: 2, z: 4, core: 2. Of those that a mesh axis runs over, the one named last changes fastest.
Arguments:
- links: float32 [4, 3, 2, 3, 3, 32, 1024], P(None, None, None, None, None, 'sa', 'ta'), may hold values from -2.5 to 2.5
- vectors: float32 [4, 16, 2, 3, 32, 1024], P('ta', None, None, None, 'sa'), may hold values from -6 to 6
Outputs:
- filtered: float32 [8, 16, 2, 3, 32, 1024], P(('cfg', 'ta'), None, None, None, 'sa'), parts along dimension 0
- grams: float32 [8, 2, 2, 16, 16], P(('cfg', 'ta')), parts along dimension 0
The draws below stay inside these ranges and needn't reach their ends.
There are 2 independent parts, one for each index of `cfg`. The reference program is written for one: setup_inputs(seed, part) draws one part's arguments, and reference() takes and returns one part's arrays. A program takes and returns all parts, laid end to end along the dimension named above; an argument that names none is the same for every part. Nothing has to cross between parts.
All inputs are finite; a program needn't handle non-finite values.
Results may differ from the reference program's by a relative error of at most 0.00011.
Values sent between devices are 32-bit elements; how exact they have to be, the bound alone decides.
A program may use at most 256 MiB of HBM per device.

```python
import jax
import jax.numpy as jnp
from jax import lax

LX = 32
LY = 32
LZ = 32
NVEC = 16
DEG = 3
NT = 4


def block_levels(key, shape, pieces, smallest, largest):
    gain, own = 1.0, jax.random.fold_in(key, 6)
    for dim, blocks in pieces:
        draws = jnp.exp(jax.random.uniform(jax.random.fold_in(own, dim), (blocks,), jnp.float32, smallest / len(pieces), largest / len(pieces)))
        gain = gain * jnp.repeat(draws, shape[dim] // blocks).reshape([-1 if axis == dim else 1 for axis in range(len(shape))])
    return gain


def gaussian(own_key, extent, spread, bound, cuts=(), dtype=jnp.bfloat16):
    entries = spread * jax.random.normal(own_key, extent, jnp.float32)
    if cuts:
        entries = entries * block_levels(own_key, extent, cuts, -0.22, 0.18)
    return jnp.clip(entries, -bound, bound).astype(dtype)


def setup_inputs(seed: int = 0, part: int = 0) -> dict:
    key_list = jax.random.split(jax.random.key(seed), 3)
    return {
        "links": gaussian(key_list[0], (NT, 3, 2, 3, 3, LZ, LY * LX), 0.41, 2.5, ((5, 8), (6, 2)), jnp.float32),
        "vectors": gaussian(key_list[1], (NT, NVEC, 2, 3, LZ, LY * LX), 1.0, 6.0, ((0, 2), (4, 8)), jnp.float32),
    }


def mat_vec(matrix, field):
    mat_re = matrix[:, None, 0]
    mat_im = matrix[:, None, 1]
    vec_re = field[:, :, 0][:, :, None]
    vec_im = field[:, :, 1][:, :, None]
    real_part = lax.optimization_barrier(jnp.sum(mat_re * vec_re - mat_im * vec_im, axis=3))
    imag_part = lax.optimization_barrier(jnp.sum(mat_re * vec_im + mat_im * vec_re, axis=3))
    return jnp.stack([real_part, imag_part], axis=2)

def adjoint(matrix):
    return jnp.stack([jnp.swapaxes(matrix[:, 0], 1, 2), -jnp.swapaxes(matrix[:, 1], 1, 2)], axis=1)

def plane_roll(array, offset, direction):
    shape = array.shape
    grid = array.reshape(shape[:-1] + (-1, LX))
    rolled = jnp.roll(grid, offset, axis=-1 if direction == 0 else -2)
    return rolled.reshape(shape)

def site_shift(array, offset, direction):
    if direction == 2:
        return jnp.roll(array, offset, axis=4)
    return plane_roll(array, offset, direction)

def hopping(links, field):
    total = jnp.zeros(field.shape, jnp.float32)
    for direction in range(3):
        matrix = links[:, direction]
        forward = mat_vec(matrix, site_shift(field, -1, direction))
        backward = site_shift(mat_vec(adjoint(matrix), field), 1, direction)
        total = total + forward
        total = total + backward
    return total

def operator(links, field):
    return 6.0 * field - hopping(links, field)

def scaled_apply(links, field):
    return (operator(links, field) - 7.0 * field) / 5.5

def gram_pair(left, right):
    count_t, count_n = (left.shape[0], left.shape[1])
    left_flat = left.reshape(count_t, count_n, 2, -1)
    right_flat = right.reshape(count_t, count_n, 2, -1)

    def inner(first, second):
        return jnp.einsum('tik,tjk->tij', first, second, precision=lax.Precision.HIGHEST)
    real_part = inner(left_flat[:, :, 0], right_flat[:, :, 0]) + inner(left_flat[:, :, 1], right_flat[:, :, 1])
    imag_part = inner(left_flat[:, :, 0], right_flat[:, :, 1]) - inner(left_flat[:, :, 1], right_flat[:, :, 0])
    return (real_part, imag_part)

def reference(links, vectors):
    previous = vectors
    current = scaled_apply(links, vectors)

    def advance(turn, carry):
        older, newer = carry
        return (newer, 2.0 * scaled_apply(links, newer) - older)
    previous, current = lax.fori_loop(0, DEG - 1, advance, (previous, current))
    sumsq = lax.optimization_barrier(jnp.sum(current * current, axis=(2, 3, 4, 5)))
    inverse = lax.rsqrt(sumsq)
    filtered = current * inverse[:, :, None, None, None, None]
    image = operator(links, filtered)
    over_re, over_im = gram_pair(filtered, filtered)
    lap_re, lap_im = gram_pair(filtered, image)
    grams = jnp.stack([jnp.stack([over_re, over_im], axis=1), jnp.stack([lap_re, lap_im], axis=1)], axis=1)
    return (filtered, grams)
```

```python
import functools

import jax
import jax.numpy as jnp
from jax import lax
from jax.experimental import pallas as pl
from jax.experimental.pallas import tpu as pltpu
from jax.sharding import PartitionSpec as P

LX = 32
DEG = 3
LANES = 128
TILE = 8
F32 = jnp.float32


def from_behind(x, axis, by):
    devices = lax.axis_size(axis)
    return lax.ppermute(x, axis, [(i, (i + by) % devices) for i in range(devices)])


def butterfly(x, axis):
    devices = lax.axis_size(axis)
    if devices & (devices - 1):
        return lax.psum(x, axis)
    step = 1
    while step < devices:
        x = x + lax.ppermute(x, axis, [(i, i ^ step) for i in range(devices)])
        step *= 2
    return x


def iota(dim):
    return lax.broadcasted_iota(jnp.int32, (TILE, LANES), dim)


def rows_at(get, total, start):
    if 0 <= start and start + TILE <= total:
        return get(start, TILE)
    base = (start // TILE) * TILE
    offset = start - base
    first, second = get(base % total, TILE), get((base + TILE) % total, TILE)
    return pltpu.roll(jnp.where(iota(0) < offset, second, first), TILE - offset, 0)


def halo_rows(get, nz, tile):
    if nz == 1:
        return get(tile * TILE, TILE)
    out = None
    for part in range(max(TILE // nz, 1)):
        row = jnp.broadcast_to(get((tile * TILE) // nz + part, 1), (TILE, LANES))
        out = row if out is None else jnp.where(iota(0) < part * nz, out, row)
    return out


def shifted(get, halo, total, nz, tile, direction, ahead):
    start, lane = tile * TILE, iota(1)
    if direction == 0:
        here = get(start, TILE)
        if ahead:
            return jnp.where(
                lane % LX == LX - 1, pltpu.roll(here, LX - 1, 1), pltpu.roll(here, LANES - 1, 1)
            )
        return jnp.where(lane % LX == 0, pltpu.roll(here, LANES - LX + 1, 1), pltpu.roll(here, 1, 1))
    if direction == 1:
        here = get(start, TILE)
        if ahead:
            other = rows_at(get, total, start + nz)
            return pltpu.roll(jnp.where(lane < LX, other, here), LANES - LX, 1)
        other = rows_at(get, total, start - nz)
        return pltpu.roll(jnp.where(lane >= LANES - LX, other, here), LX, 1)
    edge = halo_rows(halo, nz, tile)
    if nz == 1:
        return edge
    other = rows_at(get, total, start + (1 if ahead else -1))
    return jnp.where(iota(0) % nz == (nz - 1 if ahead else 0), edge, other)


def reader(ref, *index):
    return lambda start, count: ref[(*index, pl.ds(start, count), slice(None))]


def back_links_kernel(nz, links, below, out):
    total = links.shape[2]
    comps = links.shape[1] // 3

    def body(comp, carry):
        for direction in range(3):
            where = direction * comps + comp
            for tile in range(total // TILE):
                out[0, where, pl.ds(tile * TILE, TILE), :] = shifted(
                    reader(links, 0, where), reader(below, 0, comp), total, nz, tile, direction, False
                )
        return carry

    lax.fori_loop(0, comps, body, 0)


def hop(links, vec, halo, n, total, nz, tile, direction, ahead, acc):
    here = pl.ds(tile * TILE, TILE)
    for col in range(3):
        part = [
            shifted(
                reader(vec, 0, n, p * 3 + col),
                None if halo is None else reader(halo, 0, n, p * 3 + col),
                total, nz, tile, direction, ahead,
            )
            for p in range(2)
        ]
        for row in range(3):
            at = (row * 3 + col) if ahead else (col * 3 + row)
            re = links[0, direction * 18 + at, here, :]
            im = links[0, direction * 18 + 9 + at, here, :]
            if ahead:
                acc[row] = acc[row] + re * part[0] - im * part[1]
                acc[3 + row] = acc[3 + row] + re * part[1] + im * part[0]
            else:
                acc[row] = acc[row] + re * part[0] + im * part[1]
                acc[3 + row] = acc[3 + row] + re * part[1] - im * part[0]


def apply_kernel(nz, first, *refs):
    links, back, vec, low, high = refs[:5]
    prev = None if first else refs[5]
    out, top, bottom = refs[-3:]
    total = vec.shape[3]
    chunks = total // nz

    def body(n, carry):
        for tile in range(total // TILE):
            here = pl.ds(tile * TILE, TILE)
            acc = [jnp.zeros((TILE, LANES), F32)] * 6
            for direction in range(3):
                hop(links, vec, high, n, total, nz, tile, direction, True, acc)
                hop(back, vec, low, n, total, nz, tile, direction, False, acc)
            for comp in range(6):
                own = vec[0, n, comp, here, :]
                value = ((6.0 * own - acc[comp]) - 7.0 * own) * (1.0 / 5.5)
                if not first:
                    value = 2.0 * value - prev[0, n, comp, here, :]
                out[0, n, comp, here, :] = value
        for comp in range(6):
            top[0, n, comp] = out[0, n, comp, pl.ds(nz - 1, chunks, stride=nz), :]
            bottom[0, n, comp] = out[0, n, comp, pl.ds(0, chunks, stride=nz), :]
        return carry

    lax.fori_loop(0, vec.shape[1], body, 0)


def ahead_kernel(nz, links, vec, high, out):
    total = vec.shape[3]

    def body(n, carry):
        for tile in range(total // TILE):
            acc = [jnp.zeros((TILE, LANES), F32)] * 6
            for direction in range(3):
                hop(links, vec, high, n, total, nz, tile, direction, True, acc)
            for comp in range(6):
                out[0, n, comp, pl.ds(tile * TILE, TILE), :] = acc[comp]
        return carry

    lax.fori_loop(0, vec.shape[1], body, 0)


def call(kernel, args, outs, flops):
    def spec(shape):
        return pl.BlockSpec((1,) + tuple(shape[1:]), lambda t: (t,) + (0,) * (len(shape) - 1))

    moved = 4 * sum(a.size for a in args) + 4 * sum(functools.reduce(lambda x, y: x * y, o) for o in outs)
    return pl.pallas_call(
        kernel,
        grid=(args[0].shape[0],),
        in_specs=[spec(a.shape) for a in args],
        out_specs=[spec(o) for o in outs],
        out_shape=[jax.ShapeDtypeStruct(o, F32) for o in outs],
        compiler_params=pltpu.CompilerParams(vmem_limit_bytes=40 * 2**20),
        cost_estimate=pl.CostEstimate(flops=flops, bytes_accessed=moved, transcendentals=0),
    )(*args)


def to_rows(x):
    lead, (nz, sites) = x.shape[:-2], x.shape[-2:]
    x = x.reshape(lead + (nz, sites // LANES, LANES))
    return jnp.swapaxes(x, -3, -2).reshape(lead + (-1, LANES))


def from_rows(x, nz):
    lead, rows = x.shape[:-2], x.shape[-2]
    x = x.reshape(lead + (rows // nz, nz, LANES))
    return jnp.swapaxes(x, -3, -2).reshape(lead + (nz, rows // nz * LANES))


def split(x):
    high = lax.reduce_precision(x, exponent_bits=8, mantissa_bits=7)
    return high.astype(jnp.bfloat16), (x - high).astype(jnp.bfloat16)


def raw_gram(left, right):
    (lh, ll), (rh, rl) = split(left), split(right)

    def dot(a, b):
        return jnp.einsum("tipk,tjqk->tipjq", a, b, preferred_element_type=F32)

    full = dot(lh, rh) + (dot(lh, rl) + dot(ll, rh))
    return full[:, :, 0, :, 0] + full[:, :, 1, :, 1], full[:, :, 0, :, 1] - full[:, :, 1, :, 0]


def on_device(links, vectors):
    nz = vectors.shape[4]
    count_t, count_n = vectors.shape[:2]
    groups = lax.axis_size("cfg")
    me = lax.axis_index("cfg")
    own_n = count_n // groups
    pieces = 2 if own_n % 2 == 0 else 1
    part_n = own_n // pieces

    own = lax.dynamic_slice_in_dim(vectors, me * own_n, own_n, axis=1)
    own = own.reshape(own.shape[:2] + (6,) + own.shape[4:])
    own = [own[:, k * part_n : (k + 1) * part_n] for k in range(pieces)]
    lows, highs = [], []
    for field in own:
        plane = (count_t, part_n, 6, -1, LANES)
        lows.append(from_behind(field[:, :, :, nz - 1].reshape(plane), "sa", 1))
        highs.append(from_behind(field[:, :, :, 0].reshape(plane), "sa", -1))
    fields = [to_rows(field) for field in own]

    rows = to_rows(links.reshape((links.shape[0], 54) + links.shape[5:]))
    rows = lax.all_to_all(rows, "ta", split_axis=0, concat_axis=2, tiled=True)
    below = from_behind(rows[:, 36:, nz - 1 :: nz], "sa", 1)
    (back,) = call(functools.partial(back_links_kernel, nz), (rows, below), [rows.shape], rows.size * 4)

    work = fields[0].size // 6
    older = [None] * pieces
    for turn in range(DEG):
        for k in range(pieces):
            args = (rows, back, fields[k], lows[k], highs[k])
            if turn:
                args = args + (older[k],)
            new, top, bottom = call(
                functools.partial(apply_kernel, nz, turn == 0),
                args,
                [fields[k].shape, lows[k].shape, lows[k].shape],
                work * 450,
            )
            older[k], fields[k] = fields[k], new
            highs[k] = from_behind(bottom, "sa", -1)
            if turn + 1 < DEG:
                lows[k] = from_behind(top, "sa", 1)

    images = [
        call(functools.partial(ahead_kernel, nz), (rows, fields[k], highs[k]), [fields[k].shape], work * 220)[0]
        for k in range(pieces)
    ]
    field = jnp.concatenate(fields, axis=1)
    image = jnp.concatenate(images, axis=1)
    every = lax.all_gather(field, "cfg", axis=1, tiled=True)

    def flat(x):
        return x.reshape(x.shape[:2] + (2, -1))

    both = jnp.concatenate([flat(field), flat(image)], axis=1)
    re, im = raw_gram(flat(every), both)
    raw = jnp.stack([re, im], axis=1).reshape(count_t, 2, count_n, 2, own_n)
    raw = jnp.moveaxis(raw, 3, 1)
    wide = jnp.zeros((count_t, 2, 2, count_n, count_n), F32)
    raw = lax.dynamic_update_slice_in_dim(wide, raw, me * own_n, axis=4)
    raw = butterfly(butterfly(raw, "sa"), "cfg")
    over, ahead = raw[:, 0], raw[:, 1]
    turned = jnp.swapaxes(ahead, 2, 3)
    lap = 6.0 * over - jnp.stack([ahead[:, 0] + turned[:, 0], ahead[:, 1] - turned[:, 1]], axis=1)
    inverse = lax.rsqrt(jnp.diagonal(over[:, 0], axis1=1, axis2=2))
    grams = jnp.stack([over, lap], axis=1)
    grams = grams * inverse[:, None, None, :, None] * inverse[:, None, None, None, :]
    filtered = every * inverse[:, :, None, None, None]
    filtered = from_rows(filtered, nz).reshape(vectors.shape)
    return (filtered, grams)


def solution(mesh):
    in_specs = (P(None, None, None, None, None, "sa", "ta"), P("ta", None, None, None, "sa", None))
    out_specs = (
        P(("cfg", "ta"), None, None, None, "sa", None),
        P(("cfg", "ta"), None, None, None, None),
    )
    return jax.shard_map(
        on_device, mesh=mesh, in_specs=in_specs, out_specs=out_specs, check_vma=False
    )
```

```python
import functools

import jax
import jax.numpy as jnp
from jax import lax
from jax.experimental import pallas as pl
from jax.experimental.pallas import tpu as pltpu
from jax.sharding import PartitionSpec as P

LX = 32
DEG = 3
LANES = 128
TILE = 8
F32 = jnp.float32


def from_behind(x, axis, by):
    devices = lax.axis_size(axis)
    return lax.ppermute(x, axis, [(i, (i + by) % devices) for i in range(devices)])


def butterfly(x, axis):
    devices = lax.axis_size(axis)
    if devices & (devices - 1):
        return lax.psum(x, axis)
    step = 1
    while step < devices:
        x = x + lax.ppermute(x, axis, [(i, i ^ step) for i in range(devices)])
        step *= 2
    return x


def iota(dim):
    return lax.broadcasted_iota(jnp.int32, (TILE, LANES), dim)


def rows_at(get, total, start):
    if 0 <= start and start + TILE <= total:
        return get(start, TILE)
    base = (start // TILE) * TILE
    offset = start - base
    first, second = get(base % total, TILE), get((base + TILE) % total, TILE)
    return pltpu.roll(jnp.where(iota(0) < offset, second, first), TILE - offset, 0)


def halo_rows(get, nz, tile):
    if nz == 1:
        return get(tile * TILE, TILE)
    out = None
    for part in range(max(TILE // nz, 1)):
        row = jnp.broadcast_to(get((tile * TILE) // nz + part, 1), (TILE, LANES))
        out = row if out is None else jnp.where(iota(0) < part * nz, out, row)
    return out


def shifted(get, halo, total, nz, tile, direction, ahead):
    start, lane = tile * TILE, iota(1)
    if direction == 0:
        here = get(start, TILE)
        if ahead:
            return jnp.where(
                lane % LX == LX - 1, pltpu.roll(here, LX - 1, 1), pltpu.roll(here, LANES - 1, 1)
            )
        return jnp.where(lane % LX == 0, pltpu.roll(here, LANES - LX + 1, 1), pltpu.roll(here, 1, 1))
    if direction == 1:
        here = get(start, TILE)
        if ahead:
            other = rows_at(get, total, start + nz)
            return pltpu.roll(jnp.where(lane < LX, other, here), LANES - LX, 1)
        other = rows_at(get, total, start - nz)
        return pltpu.roll(jnp.where(lane >= LANES - LX, other, here), LX, 1)
    edge = halo_rows(halo, nz, tile)
    if nz == 1:
        return edge
    other = rows_at(get, total, start + (1 if ahead else -1))
    return jnp.where(iota(0) % nz == (nz - 1 if ahead else 0), edge, other)


def reader(ref, *index):
    return lambda start, count: ref[(*index, pl.ds(start, count), slice(None))]


def edges_kernel(nz, pieces, place, vec, *outs):
    own_n, total = vec.shape[1], vec.shape[3]
    chunks, part_n = total // nz, own_n // pieces
    for k in range(pieces):
        top, bottom = outs[2 * k], outs[2 * k + 1]

        def body(n, carry):
            for comp in range(6):
                top[0, n, comp] = vec[0, k * part_n + n, comp, pl.ds(nz - 1, chunks, stride=nz), :]
                bottom[0, n, comp] = vec[0, k * part_n + n, comp, pl.ds(0, chunks, stride=nz), :]
            return carry

        lax.fori_loop(0, part_n, body, 0)


def join_links_kernel(nz, place, mine, theirs, out, top):
    half = mine.shape[2]
    chunks = 2 * half // nz
    ahead = place[1] == 0

    def body(comp, carry):
        a, b = mine[0, comp], theirs[0, comp]
        out[0, comp, pl.ds(0, half), :] = jnp.where(ahead, a, b)
        out[0, comp, pl.ds(half, half), :] = jnp.where(ahead, b, a)
        return carry

    def edge(comp, carry):
        first = out.shape[1] - top.shape[1]
        top[0, comp] = out[0, first + comp, pl.ds(nz - 1, chunks, stride=nz), :]
        return carry

    lax.fori_loop(0, out.shape[1], body, 0)
    lax.fori_loop(0, top.shape[1], edge, 0)


def back_links_kernel(nz, links, below, out):
    total = links.shape[2]
    comps = links.shape[1] // 3

    def body(comp, carry):
        for direction in range(3):
            where = direction * comps + comp
            for tile in range(total // TILE):
                out[0, where, pl.ds(tile * TILE, TILE), :] = shifted(
                    reader(links, 0, where), reader(below, 0, comp), total, nz, tile, direction, False
                )
        return carry

    lax.fori_loop(0, comps, body, 0)


def scale_kernel(groups, pieces, place, inverse, *refs):
    out = refs[-1]
    t = pl.program_id(0)
    part_n = refs[0].shape[1]
    for away in range(groups):
        source = lax.rem(place[0] + away, groups)
        for k in range(pieces):
            piece = refs[away * pieces + k]
            base = (source * pieces + k) * part_n

            def body(n, carry):
                out[0, base + n] = piece[0, n] * inverse[t, base + n]
                return carry

            lax.fori_loop(0, part_n, body, 0)


def hop(links, vec, halo, n, total, nz, tile, direction, ahead, acc):
    here = pl.ds(tile * TILE, TILE)
    for col in range(3):
        part = [
            shifted(
                reader(vec, 0, n, p * 3 + col),
                None if halo is None else reader(halo, 0, n, p * 3 + col),
                total, nz, tile, direction, ahead,
            )
            for p in range(2)
        ]
        for row in range(3):
            at = (row * 3 + col) if ahead else (col * 3 + row)
            re = links[0, direction * 18 + at, here, :]
            im = links[0, direction * 18 + 9 + at, here, :]
            if ahead:
                acc[row] = acc[row] + re * part[0] - im * part[1]
                acc[3 + row] = acc[3 + row] + re * part[1] + im * part[0]
            else:
                acc[row] = acc[row] + re * part[0] + im * part[1]
                acc[3 + row] = acc[3 + row] + re * part[1] - im * part[0]


def apply_kernel(nz, first, place, *refs):
    links, back, vec, low, high = refs[:5]
    prev = None if first else refs[5]
    out, top, bottom = refs[-3:]
    total = vec.shape[3]
    chunks = total // nz

    def body(n, carry):
        for tile in range(total // TILE):
            here = pl.ds(tile * TILE, TILE)
            acc = [jnp.zeros((TILE, LANES), F32)] * 6
            for direction in range(3):
                hop(links, vec, high, n, total, nz, tile, direction, True, acc)
                hop(back, vec, low, n, total, nz, tile, direction, False, acc)
            for comp in range(6):
                own = vec[0, n, comp, here, :]
                value = ((6.0 * own - acc[comp]) - 7.0 * own) * (1.0 / 5.5)
                if not first:
                    value = 2.0 * value - prev[0, n, comp, here, :]
                out[0, n, comp, here, :] = value
        for comp in range(6):
            top[0, n, comp] = out[0, n, comp, pl.ds(nz - 1, chunks, stride=nz), :]
            bottom[0, n, comp] = out[0, n, comp, pl.ds(0, chunks, stride=nz), :]
        return carry

    lax.fori_loop(0, vec.shape[1], body, 0)


def ahead_kernel(nz, links, vec, high, out):
    total = vec.shape[3]

    def body(n, carry):
        for tile in range(total // TILE):
            acc = [jnp.zeros((TILE, LANES), F32)] * 6
            for direction in range(3):
                hop(links, vec, high, n, total, nz, tile, direction, True, acc)
            for comp in range(6):
                out[0, n, comp, pl.ds(tile * TILE, TILE), :] = acc[comp]
        return carry

    lax.fori_loop(0, vec.shape[1], body, 0)


def call(kernel, args, outs, flops=0, place=None, blocks=(), smem=()):
    blocks = dict(blocks)

    def plain(shape):
        return pl.BlockSpec((1,) + tuple(shape[1:]), lambda t, *_: (t,) + (0,) * (len(shape) - 1))

    def spec(at, arg):
        return pl.BlockSpec(*blocks[at]) if at in blocks else plain(arg.shape)

    in_specs = [pl.BlockSpec(memory_space=pltpu.SMEM)] * len(smem) + [spec(i, a) for i, a in enumerate(args)]
    moved = 8 * sum(functools.reduce(lambda x, y: x * y, o) for o in outs)
    scalars = () if place is None else (place,)
    return pl.pallas_call(
        kernel,
        grid_spec=pltpu.PrefetchScalarGridSpec(
            num_scalar_prefetch=len(scalars),
            grid=(outs[0][0],),
            in_specs=in_specs,
            out_specs=[plain(o) for o in outs],
        ),
        out_shape=[jax.ShapeDtypeStruct(o, F32) for o in outs],
        compiler_params=pltpu.CompilerParams(vmem_limit_bytes=40 * 2**20),
        cost_estimate=pl.CostEstimate(flops=flops, bytes_accessed=moved, transcendentals=0),
    )(*scalars, *smem, *args)


def to_rows(x):
    lead, (nz, sites) = x.shape[:-2], x.shape[-2:]
    x = x.reshape(lead + (nz, sites // LANES, LANES))
    return jnp.swapaxes(x, -3, -2).reshape(lead + (-1, LANES))


def from_rows(x, nz):
    lead, rows = x.shape[:-2], x.shape[-2]
    x = x.reshape(lead + (rows // nz, nz, LANES))
    return jnp.swapaxes(x, -3, -2).reshape(lead + (nz, rows // nz * LANES))


def split(x):
    high = lax.reduce_precision(x, exponent_bits=8, mantissa_bits=7)
    return high.astype(jnp.bfloat16), (x - high).astype(jnp.bfloat16)


def raw_gram(left, right):
    (lh, ll), (rh, rl) = split(left), split(right)

    def dot(a, b):
        return jnp.einsum("tipk,tjqk->tipjq", a, b, preferred_element_type=F32)

    full = dot(lh, rh) + (dot(lh, rl) + dot(ll, rh))
    return full[:, :, 0, :, 0] + full[:, :, 1, :, 1], full[:, :, 0, :, 1] - full[:, :, 1, :, 0]


def join_links(links, place, nz):
    rows = to_rows(links.reshape((links.shape[0], 54) + links.shape[5:]))
    count = lax.axis_size("ta")
    if count != 2:
        rows = lax.all_to_all(rows, "ta", split_axis=0, concat_axis=2, tiled=True)
        return rows, rows[:, 36:, nz - 1 :: nz]
    half = rows.shape[0] // 2
    sent = lax.dynamic_slice_in_dim(rows, (1 - place[1]) * half, half, axis=0)
    theirs = from_behind(sent, "ta", 1)
    total = 2 * rows.shape[2]
    block = ((1,) + rows.shape[1:], lambda t, place: (place[1] * half + t, 0, 0, 0))
    return call(
        functools.partial(join_links_kernel, nz),
        (rows, theirs),
        [(half, 54, total, LANES), (half, 18, total // nz, LANES)],
        place=place,
        blocks={0: block},
    )


def on_device(links, vectors):
    nz = vectors.shape[4]
    count_t, count_n = vectors.shape[:2]
    groups = lax.axis_size("cfg")
    me = lax.axis_index("cfg")
    place = jnp.stack([me, lax.axis_index("ta")]).astype(jnp.int32)
    own_n = count_n // groups
    pieces = 2 if own_n % 2 == 0 else 1
    part_n = own_n // pieces

    every = to_rows(vectors.reshape((count_t, count_n, 6) + vectors.shape[4:]))
    total = every.shape[3]
    shape = (count_t, part_n, 6, total, LANES)
    edge = (count_t, part_n, 6, total // nz, LANES)
    own_block = ((1, own_n) + every.shape[2:], lambda t, place: (t, place[0], 0, 0, 0))
    edges = call(
        functools.partial(edges_kernel, nz, pieces), (every,), [edge] * (2 * pieces), place=place, blocks={0: own_block}
    )
    lows = [from_behind(edges[2 * k], "sa", 1) for k in range(pieces)]
    highs = [from_behind(edges[2 * k + 1], "sa", -1) for k in range(pieces)]

    rows, top_links = join_links(links, place, nz)
    below = from_behind(top_links, "sa", 1)
    (back,) = call(functools.partial(back_links_kernel, nz), (rows, below), [rows.shape], rows.size * 4)

    work = count_t * part_n * total * LANES
    fields, older = [every] * pieces, [None] * pieces

    def part(k):
        return ((1, part_n) + every.shape[2:], lambda t, place: (t, place[0] * pieces + k, 0, 0, 0))

    for turn in range(DEG):
        for k in range(pieces):
            args, blocks = (rows, back, fields[k], lows[k], highs[k]), {}
            if turn:
                args = args + (older[k],)
            if turn == 0:
                blocks[2] = part(k)
            if turn == 1:
                blocks[5] = part(k)
            new, top, bottom = call(
                functools.partial(apply_kernel, nz, turn == 0),
                args,
                [shape, edge, edge],
                work * 450,
                place,
                blocks,
            )
            older[k], fields[k] = fields[k], new
            highs[k] = from_behind(bottom, "sa", -1)
            if turn + 1 < DEG:
                lows[k] = from_behind(top, "sa", 1)

    held = [fields] + [[from_behind(f, "cfg", -away) for f in fields] for away in range(1, groups)]
    sums = jnp.concatenate([jnp.sum(f * f, axis=(2, 3, 4)) for f in fields], axis=1)
    sums = lax.dynamic_update_slice_in_dim(jnp.zeros((count_t, count_n), F32), sums, me * own_n, axis=1)
    inverse = lax.rsqrt(butterfly(butterfly(sums, "sa"), "cfg"))

    images = [
        call(functools.partial(ahead_kernel, nz), (rows, fields[k], highs[k]), [shape], work * 220)[0]
        for k in range(pieces)
    ]

    def flat(x):
        return x.reshape(x.shape[:2] + (2, -1))

    both = jnp.concatenate([flat(x) for x in fields + images], axis=1)
    raw = jnp.zeros((count_t, 2, 2, count_n, count_n), F32)
    for away in range(groups):
        source = lax.rem(me + away, groups)
        for k in range(pieces):
            re, im = raw_gram(flat(held[away][k]), both)
            block = jnp.stack([re, im], axis=1).reshape(count_t, 2, part_n, 2, own_n)
            block = jnp.moveaxis(block, 3, 1)
            raw = lax.dynamic_update_slice(raw, block, (0, 0, 0, source * own_n + k * part_n, me * own_n))
    raw = butterfly(butterfly(raw, "sa"), "cfg")
    over, ahead = raw[:, 0], raw[:, 1]
    turned = jnp.swapaxes(ahead, 2, 3)
    lap = 6.0 * over - jnp.stack([ahead[:, 0] + turned[:, 0], ahead[:, 1] - turned[:, 1]], axis=1)
    grams = jnp.stack([over, lap], axis=1)
    grams = grams * inverse[:, None, None, :, None] * inverse[:, None, None, None, :]
    (filtered,) = call(
        functools.partial(scale_kernel, groups, pieces),
        [piece for source in held for piece in source],
        [every.shape],
        place=place,
        smem=(inverse,),
    )
    return (from_rows(filtered, nz).reshape(vectors.shape), grams)


def solution(mesh):
    in_specs = (P(None, None, None, None, None, "sa", "ta"), P("ta", None, None, None, "sa", None))
    out_specs = (
        P(("cfg", "ta"), None, None, None, "sa", None),
        P(("cfg", "ta"), None, None, None, None),
    )
    return jax.shard_map(
        on_device, mesh=mesh, in_specs=in_specs, out_specs=out_specs, check_vma=False
    )
```

```python
import functools

import jax
import jax.numpy as jnp
from jax import lax
from jax.experimental import pallas as pl
from jax.experimental.pallas import tpu as pltpu
from jax.sharding import PartitionSpec as P

LX = 32
DEG = 3
LANES = 128
TILE = 8
F32 = jnp.float32


def from_behind(x, axis, by):
    devices = lax.axis_size(axis)
    return lax.ppermute(x, axis, [(i, (i + by) % devices) for i in range(devices)])


def iota(dim):
    return lax.broadcasted_iota(jnp.int32, (TILE, LANES), dim)


def rows_at(get, total, start):
    if 0 <= start and start + TILE <= total:
        return get(start, TILE)
    base = (start // TILE) * TILE
    offset = start - base
    first, second = get(base % total, TILE), get((base + TILE) % total, TILE)
    return pltpu.roll(jnp.where(iota(0) < offset, second, first), TILE - offset, 0)


def halo_rows(get, nz, tile):
    if nz == 1:
        return get(tile * TILE, TILE)
    out = None
    for part in range(max(TILE // nz, 1)):
        row = jnp.broadcast_to(get((tile * TILE) // nz + part, 1), (TILE, LANES))
        out = row if out is None else jnp.where(iota(0) < part * nz, out, row)
    return out


def shifted(get, halo, total, nz, tile, direction, ahead):
    start, lane = tile * TILE, iota(1)
    if direction == 0:
        here = get(start, TILE)
        if ahead:
            return jnp.where(
                lane % LX == LX - 1, pltpu.roll(here, LX - 1, 1), pltpu.roll(here, LANES - 1, 1)
            )
        return jnp.where(lane % LX == 0, pltpu.roll(here, LANES - LX + 1, 1), pltpu.roll(here, 1, 1))
    if direction == 1:
        here = get(start, TILE)
        if ahead:
            other = rows_at(get, total, start + nz)
            return pltpu.roll(jnp.where(lane < LX, other, here), LANES - LX, 1)
        other = rows_at(get, total, start - nz)
        return pltpu.roll(jnp.where(lane >= LANES - LX, other, here), LX, 1)
    edge = halo_rows(halo, nz, tile)
    if nz == 1:
        return edge
    other = rows_at(get, total, start + (1 if ahead else -1))
    return jnp.where(iota(0) % nz == (nz - 1 if ahead else 0), edge, other)


def reader(ref, *index):
    return lambda start, count: ref[(*index, pl.ds(start, count), slice(None))]


def edges_kernel(nz, pieces, place, vec, *outs):
    own_n, total = vec.shape[1], vec.shape[3]
    chunks, part_n = total // nz, own_n // pieces
    for k in range(pieces):
        top, bottom = outs[2 * k], outs[2 * k + 1]

        def body(n, carry):
            for comp in range(6):
                top[0, n, comp] = vec[0, k * part_n + n, comp, pl.ds(nz - 1, chunks, stride=nz), :]
                bottom[0, n, comp] = vec[0, k * part_n + n, comp, pl.ds(0, chunks, stride=nz), :]
            return carry

        lax.fori_loop(0, part_n, body, 0)


def join_links_kernel(nz, place, mine, theirs, out, top):
    half = mine.shape[2]
    chunks = 2 * half // nz
    ahead = place[1] == 0

    def body(comp, carry):
        a, b = mine[0, comp], theirs[0, comp]
        out[0, comp, pl.ds(0, half), :] = jnp.where(ahead, a, b)
        out[0, comp, pl.ds(half, half), :] = jnp.where(ahead, b, a)
        return carry

    def edge(comp, carry):
        first = out.shape[1] - top.shape[1]
        top[0, comp] = out[0, first + comp, pl.ds(nz - 1, chunks, stride=nz), :]
        return carry

    lax.fori_loop(0, out.shape[1], body, 0)
    lax.fori_loop(0, top.shape[1], edge, 0)


def back_links_kernel(nz, links, below, out):
    total = links.shape[2]
    comps = links.shape[1] // 3

    def body(comp, carry):
        for direction in range(3):
            where = direction * comps + comp
            for tile in range(total // TILE):
                out[0, where, pl.ds(tile * TILE, TILE), :] = shifted(
                    reader(links, 0, where), reader(below, 0, comp), total, nz, tile, direction, False
                )
        return carry

    lax.fori_loop(0, comps, body, 0)


def scale_kernel(groups, pieces, place, inverse, *refs):
    out = refs[-1]
    t = pl.program_id(0)
    part_n = refs[0].shape[1]
    for away in range(groups):
        source = lax.rem(place[0] + away, groups)
        for k in range(pieces):
            piece = refs[away * pieces + k]
            base = (source * pieces + k) * part_n

            def body(n, carry):
                out[0, base + n] = piece[0, n] * inverse[t, base + n]
                return carry

            lax.fori_loop(0, part_n, body, 0)


def hop(links, vec, halo, n, total, nz, tile, direction, ahead, acc):
    here = pl.ds(tile * TILE, TILE)
    for col in range(3):
        part = [
            shifted(
                reader(vec, 0, n, p * 3 + col),
                None if halo is None else reader(halo, 0, n, p * 3 + col),
                total, nz, tile, direction, ahead,
            )
            for p in range(2)
        ]
        for row in range(3):
            at = (row * 3 + col) if ahead else (col * 3 + row)
            re = links[0, direction * 18 + at, here, :]
            im = links[0, direction * 18 + 9 + at, here, :]
            if ahead:
                acc[row] = acc[row] + re * part[0] - im * part[1]
                acc[3 + row] = acc[3 + row] + re * part[1] + im * part[0]
            else:
                acc[row] = acc[row] + re * part[0] + im * part[1]
                acc[3 + row] = acc[3 + row] + re * part[1] - im * part[0]


def apply_kernel(nz, first, place, *refs):
    links, back, vec, low, high = refs[:5]
    prev = None if first else refs[5]
    out, top, bottom = refs[-3:]
    total = vec.shape[3]
    chunks = total // nz

    def body(n, carry):
        for tile in range(total // TILE):
            here = pl.ds(tile * TILE, TILE)
            acc = [jnp.zeros((TILE, LANES), F32)] * 6
            for direction in range(3):
                hop(links, vec, high, n, total, nz, tile, direction, True, acc)
                hop(back, vec, low, n, total, nz, tile, direction, False, acc)
            for comp in range(6):
                own = vec[0, n, comp, here, :]
                value = ((6.0 * own - acc[comp]) - 7.0 * own) * (1.0 / 5.5)
                if not first:
                    value = 2.0 * value - prev[0, n, comp, here, :]
                out[0, n, comp, here, :] = value
        for comp in range(6):
            top[0, n, comp] = out[0, n, comp, pl.ds(nz - 1, chunks, stride=nz), :]
            bottom[0, n, comp] = out[0, n, comp, pl.ds(0, chunks, stride=nz), :]
        return carry

    lax.fori_loop(0, vec.shape[1], body, 0)


def ahead_kernel(nz, links, vec, high, out):
    total = vec.shape[3]

    def body(n, carry):
        for tile in range(total // TILE):
            acc = [jnp.zeros((TILE, LANES), F32)] * 6
            for direction in range(3):
                hop(links, vec, high, n, total, nz, tile, direction, True, acc)
            for comp in range(6):
                out[0, n, comp, pl.ds(tile * TILE, TILE), :] = acc[comp]
        return carry

    lax.fori_loop(0, vec.shape[1], body, 0)


def gram_kernel(count, *refs):
    left, right, out, total = refs[:count], refs[count:-2], refs[-2], refs[-1]
    tiles = left[0].shape[3] // TILE
    wide = 2 if tiles % 2 == 0 else 1

    def gather(pieces, colour, first):
        rows = []
        for p in range(2):
            for piece in pieces:
                lanes = [
                    piece[0, :, p * 3 + colour, pl.ds((first + j) * TILE, TILE), :].reshape(-1, LANES)
                    for j in range(wide)
                ]
                rows.append(jnp.concatenate(lanes, axis=1) if wide > 1 else lanes[0])
        value = jnp.concatenate(rows, axis=0)
        high = value.astype(jnp.bfloat16)
        return high, (value - high.astype(F32)).astype(jnp.bfloat16)

    def dot(a, b):
        return lax.dot_general(a, b, (((1,), (1,)), ((), ())), preferred_element_type=F32)

    total[...] = jnp.zeros_like(total)
    for colour in range(3):
        for first in range(0, tiles, wide):
            lh, ll = gather(left, colour, first)
            rh, rl = gather(right, colour, first)
            total[...] += dot(lh, rh) + (dot(lh, rl) + dot(ll, rh))

    rows, cols = total.shape
    at_row = lax.broadcasted_iota(jnp.int32, (rows, cols), 0) % TILE
    at_col = lax.broadcasted_iota(jnp.int32, (rows, cols), 1) % TILE
    value = jnp.where(at_row == at_col, total[...], 0.0)

    def picks(n):
        i = lax.broadcasted_iota(jnp.int32, (n // TILE, n), 0)
        j = lax.broadcasted_iota(jnp.int32, (n // TILE, n), 1)
        return jnp.where(j // TILE == i, 1.0, 0.0)

    value = jnp.dot(picks(rows), value, precision=lax.Precision.HIGHEST, preferred_element_type=F32)
    out[0] = lax.dot_general(
        value, picks(cols), (((1,), (1,)), ((), ())),
        precision=lax.Precision.HIGHEST, preferred_element_type=F32,
    )


def sum_kernel(groups, size, mine, out, slots, send_sem, recv_sem):
    count = groups * size
    me = lax.axis_index("cfg") * size + lax.axis_index("sa")

    def device(away):
        other = lax.rem(me + away, count)
        return {"cfg": other // size, "sa": lax.rem(other, size)}

    barrier = pltpu.get_barrier_semaphore()
    for away in range(1, count):
        pl.semaphore_signal(barrier, inc=1, device_id=device(away), device_id_type=pl.DeviceIdType.MESH)
    pl.semaphore_wait(barrier, count - 1)
    copies = []
    for away in range(1, count):
        copy = pltpu.make_async_remote_copy(
            src_ref=mine,
            dst_ref=slots.at[away],
            send_sem=send_sem.at[away],
            recv_sem=recv_sem.at[away],
            device_id=device(away),
            device_id_type=pl.DeviceIdType.MESH,
        )
        copy.start()
        copies.append(copy)
    slots[0] = mine[...]
    for copy in copies:
        copy.wait()
    for group in range(groups):
        value = slots[lax.rem(me + count - group * size, count)]
        for source in range(1, size):
            value = value + slots[lax.rem(me + 2 * count - group * size - source, count)]
        out[group] = value


def sum_blocks(block, groups, size):
    count = groups * size
    return pl.pallas_call(
        functools.partial(sum_kernel, groups, size),
        out_shape=jax.ShapeDtypeStruct((groups,) + block.shape, F32),
        in_specs=[pl.BlockSpec(memory_space=pltpu.VMEM)],
        out_specs=pl.BlockSpec(memory_space=pltpu.VMEM),
        scratch_shapes=[
            pltpu.VMEM((count,) + block.shape, F32),
            pltpu.SemaphoreType.DMA((count,)),
            pltpu.SemaphoreType.DMA((count,)),
        ],
        compiler_params=pltpu.CompilerParams(
            collective_id=0, has_side_effects=True, vmem_limit_bytes=40 * 2**20
        ),
    )(block)


def call(kernel, args, outs, flops=0, place=None, blocks=(), smem=(), scratch=()):
    blocks = dict(blocks)

    def plain(shape):
        return pl.BlockSpec((1,) + tuple(shape[1:]), lambda t, *_: (t,) + (0,) * (len(shape) - 1))

    def spec(at, arg):
        return pl.BlockSpec(*blocks[at]) if at in blocks else plain(arg.shape)

    in_specs = [pl.BlockSpec(memory_space=pltpu.SMEM)] * len(smem) + [spec(i, a) for i, a in enumerate(args)]
    moved = 8 * sum(functools.reduce(lambda x, y: x * y, o) for o in outs)
    scalars = () if place is None else (place,)
    return pl.pallas_call(
        kernel,
        grid_spec=pltpu.PrefetchScalarGridSpec(
            num_scalar_prefetch=len(scalars),
            grid=(outs[0][0],),
            in_specs=in_specs,
            out_specs=[plain(o) for o in outs],
            scratch_shapes=list(scratch),
        ),
        out_shape=[jax.ShapeDtypeStruct(o, F32) for o in outs],
        compiler_params=pltpu.CompilerParams(vmem_limit_bytes=40 * 2**20),
        cost_estimate=pl.CostEstimate(flops=flops, bytes_accessed=moved, transcendentals=0),
    )(*scalars, *smem, *args)


def to_rows(x):
    lead, (nz, sites) = x.shape[:-2], x.shape[-2:]
    x = x.reshape(lead + (nz, sites // LANES, LANES))
    return jnp.swapaxes(x, -3, -2).reshape(lead + (-1, LANES))


def from_rows(x, nz):
    lead, rows = x.shape[:-2], x.shape[-2]
    x = x.reshape(lead + (rows // nz, nz, LANES))
    return jnp.swapaxes(x, -3, -2).reshape(lead + (nz, rows // nz * LANES))


def join_links(links, place, nz):
    rows = to_rows(links.reshape((links.shape[0], 54) + links.shape[5:]))
    count = lax.axis_size("ta")
    if count != 2:
        rows = lax.all_to_all(rows, "ta", split_axis=0, concat_axis=2, tiled=True)
        return rows, rows[:, 36:, nz - 1 :: nz]
    half = rows.shape[0] // 2
    sent = lax.dynamic_slice_in_dim(rows, (1 - place[1]) * half, half, axis=0)
    theirs = from_behind(sent, "ta", 1)
    total = 2 * rows.shape[2]
    block = ((1,) + rows.shape[1:], lambda t, place: (place[1] * half + t, 0, 0, 0))
    return call(
        functools.partial(join_links_kernel, nz),
        (rows, theirs),
        [(half, 54, total, LANES), (half, 18, total // nz, LANES)],
        place=place,
        blocks={0: block},
    )


def on_device(links, vectors):
    nz = vectors.shape[4]
    count_t, count_n = vectors.shape[:2]
    groups = lax.axis_size("cfg")
    me = lax.axis_index("cfg")
    place = jnp.stack([me, lax.axis_index("ta")]).astype(jnp.int32)
    own_n = count_n // groups
    pieces = 2 if own_n % 2 == 0 else 1
    part_n = own_n // pieces

    every = to_rows(vectors.reshape((count_t, count_n, 6) + vectors.shape[4:]))
    total = every.shape[3]
    shape = (count_t, part_n, 6, total, LANES)
    edge = (count_t, part_n, 6, total // nz, LANES)
    own_block = ((1, own_n) + every.shape[2:], lambda t, place: (t, place[0], 0, 0, 0))
    edges = call(
        functools.partial(edges_kernel, nz, pieces), (every,), [edge] * (2 * pieces), place=place, blocks={0: own_block}
    )
    lows = [from_behind(edges[2 * k], "sa", 1) for k in range(pieces)]
    highs = [from_behind(edges[2 * k + 1], "sa", -1) for k in range(pieces)]

    rows, top_links = join_links(links, place, nz)
    below = from_behind(top_links, "sa", 1)
    (back,) = call(functools.partial(back_links_kernel, nz), (rows, below), [rows.shape], rows.size * 4)

    work = count_t * part_n * total * LANES
    fields, older = [every] * pieces, [None] * pieces

    def part(k):
        return ((1, part_n) + every.shape[2:], lambda t, place: (t, place[0] * pieces + k, 0, 0, 0))

    for turn in range(DEG):
        for k in range(pieces):
            args, blocks = (rows, back, fields[k], lows[k], highs[k]), {}
            if turn:
                args = args + (older[k],)
            if turn == 0:
                blocks[2] = part(k)
            if turn == 1:
                blocks[5] = part(k)
            new, top, bottom = call(
                functools.partial(apply_kernel, nz, turn == 0),
                args,
                [shape, edge, edge],
                work * 450,
                place,
                blocks,
            )
            older[k], fields[k] = fields[k], new
            highs[k] = from_behind(bottom, "sa", -1)
            if turn + 1 < DEG:
                lows[k] = from_behind(top, "sa", 1)

    held = [fields] + [[from_behind(f, "cfg", -away) for f in fields] for away in range(1, groups)]
    images = [
        call(functools.partial(ahead_kernel, nz), (rows, fields[k], highs[k]), [shape], work * 220)[0]
        for k in range(pieces)
    ]

    right = fields + images
    side, across = 2 * own_n, 2 * 2 * own_n
    grams = [
        call(
            functools.partial(gram_kernel, pieces),
            held[away] + right,
            [(count_t, side, across)],
            2 * 3 * side * TILE * across * work // part_n,
            scratch=[pltpu.VMEM((side * TILE, across * TILE), F32)],
        )[0]
        for away in range(groups)
    ]
    block = jnp.stack(grams).reshape(-1, LANES)
    raw = sum_blocks(block, groups, lax.axis_size("sa"))
    raw = raw.reshape(groups, groups, count_t, 2, own_n, 2, 2, own_n)
    re = raw[:, :, :, 0, :, 0] + raw[:, :, :, 1, :, 1]
    im = raw[:, :, :, 0, :, 1] - raw[:, :, :, 1, :, 0]
    raw = jnp.moveaxis(jnp.stack([re, im], axis=3), 5, 3)
    raw = jnp.concatenate(
        [
            jnp.concatenate([raw[g, (source - g) % groups] for source in range(groups)], axis=3)
            for g in range(groups)
        ],
        axis=4,
    )
    over, ahead = raw[:, 0], raw[:, 1]
    own_entry = jnp.eye(count_n, dtype=bool)
    inverse = lax.rsqrt(jnp.sum(jnp.where(own_entry, over[:, 0], 0.0), axis=2))
    turned = jnp.swapaxes(ahead, 2, 3)
    lap = 6.0 * over - jnp.stack([ahead[:, 0] + turned[:, 0], ahead[:, 1] - turned[:, 1]], axis=1)
    grams = jnp.stack([over, lap], axis=1)
    grams = grams * inverse[:, None, None, :, None] * inverse[:, None, None, None, :]
    (filtered,) = call(
        functools.partial(scale_kernel, groups, pieces),
        [piece for source in held for piece in source],
        [every.shape],
        place=place,
        smem=(inverse,),
    )
    return (from_rows(filtered, nz).reshape(vectors.shape), grams)


def solution(mesh):
    in_specs = (P(None, None, None, None, None, "sa", "ta"), P("ta", None, None, None, "sa", None))
    out_specs = (
        P(("cfg", "ta"), None, None, None, "sa", None),
        P(("cfg", "ta"), None, None, None, None),
    )
    return jax.shard_map(
        on_device, mesh=mesh, in_specs=in_specs, out_specs=out_specs, check_vma=False
    )
```

```python
import functools

import jax
import jax.numpy as jnp
from jax import lax
from jax.experimental import pallas as pl
from jax.experimental.pallas import tpu as pltpu
from jax.sharding import PartitionSpec as P

LX = 32
DEG = 3
LANES = 128
TILE = 8
F32 = jnp.float32


def from_behind(x, axis, by):
    devices = lax.axis_size(axis)
    return lax.ppermute(x, axis, [(i, (i + by) % devices) for i in range(devices)])


def iota(dim):
    return lax.broadcasted_iota(jnp.int32, (TILE, LANES), dim)


def rows_at(get, total, start):
    if 0 <= start and start + TILE <= total:
        return get(start, TILE)
    base = (start // TILE) * TILE
    offset = start - base
    first, second = get(base % total, TILE), get((base + TILE) % total, TILE)
    return pltpu.roll(jnp.where(iota(0) < offset, second, first), TILE - offset, 0)


def halo_rows(get, nz, tile):
    if nz == 1:
        return get(tile * TILE, TILE)
    out = None
    for part in range(max(TILE // nz, 1)):
        row = jnp.broadcast_to(get((tile * TILE) // nz + part, 1), (TILE, LANES))
        out = row if out is None else jnp.where(iota(0) < part * nz, out, row)
    return out


def shifted(get, halo, total, nz, tile, direction, ahead):
    start, lane = tile * TILE, iota(1)
    if direction == 0:
        here = get(start, TILE)
        if ahead:
            return jnp.where(
                lane % LX == LX - 1, pltpu.roll(here, LX - 1, 1), pltpu.roll(here, LANES - 1, 1)
            )
        return jnp.where(lane % LX == 0, pltpu.roll(here, LANES - LX + 1, 1), pltpu.roll(here, 1, 1))
    if direction == 1:
        here = get(start, TILE)
        if ahead:
            other = rows_at(get, total, start + nz)
            return pltpu.roll(jnp.where(lane < LX, other, here), LANES - LX, 1)
        other = rows_at(get, total, start - nz)
        return pltpu.roll(jnp.where(lane >= LANES - LX, other, here), LX, 1)
    edge = halo_rows(halo, nz, tile)
    if nz == 1:
        return edge
    other = rows_at(get, total, start + (1 if ahead else -1))
    return jnp.where(iota(0) % nz == (nz - 1 if ahead else 0), edge, other)


def reader(ref, *index):
    return lambda start, count: ref[(*index, pl.ds(start, count), slice(None))]


def edges_kernel(nz, pieces, place, vec, *outs):
    own_n, total = vec.shape[1], vec.shape[3]
    chunks, part_n = total // nz, own_n // pieces
    for k in range(pieces):
        top, bottom = outs[2 * k], outs[2 * k + 1]

        def body(n, carry):
            for comp in range(6):
                top[0, n, comp] = vec[0, k * part_n + n, comp, pl.ds(nz - 1, chunks, stride=nz), :]
                bottom[0, n, comp] = vec[0, k * part_n + n, comp, pl.ds(0, chunks, stride=nz), :]
            return carry

        lax.fori_loop(0, part_n, body, 0)


def join_links_kernel(nz, place, mine, theirs, below_mine, below_theirs, out, back, below):
    half, edge = mine.shape[2], below_mine.shape[2]
    total, comps = out.shape[2], out.shape[1] // 3
    ahead = place[1] == 0

    def join(comp, carry):
        a, b = mine[0, comp], theirs[0, comp]
        out[0, comp, pl.ds(0, half), :] = jnp.where(ahead, a, b)
        out[0, comp, pl.ds(half, half), :] = jnp.where(ahead, b, a)
        return carry

    def join_edge(comp, carry):
        a, b = below_mine[0, comp], below_theirs[0, comp]
        below[0, comp, pl.ds(0, edge), :] = jnp.where(ahead, a, b)
        below[0, comp, pl.ds(edge, edge), :] = jnp.where(ahead, b, a)
        return carry

    def body(comp, carry):
        for direction in range(3):
            where = direction * comps + comp
            for tile in range(total // TILE):
                back[0, where, pl.ds(tile * TILE, TILE), :] = shifted(
                    reader(out, 0, where), reader(below, 0, comp), total, nz, tile, direction, False
                )
        return carry

    lax.fori_loop(0, out.shape[1], join, 0)
    lax.fori_loop(0, comps, join_edge, 0)
    lax.fori_loop(0, comps, body, 0)


def scale_kernel(groups, pieces, place, inverse, *refs):
    out = refs[-1]
    t = pl.program_id(0)
    part_n = refs[0].shape[1]
    for away in range(groups):
        source = lax.rem(place[0] + away, groups)
        for k in range(pieces):
            piece = refs[away * pieces + k]
            base = (source * pieces + k) * part_n

            def body(n, carry):
                out[0, base + n] = piece[0, n] * inverse[t, base + n]
                return carry

            lax.fori_loop(0, part_n, body, 0)


def hop(links, vec, halo, n, total, nz, tile, direction, ahead, acc):
    here = pl.ds(tile * TILE, TILE)
    for col in range(3):
        part = [
            shifted(
                reader(vec, 0, n, p * 3 + col),
                None if halo is None else reader(halo, 0, n, p * 3 + col),
                total, nz, tile, direction, ahead,
            )
            for p in range(2)
        ]
        for row in range(3):
            at = (row * 3 + col) if ahead else (col * 3 + row)
            re = links[0, direction * 18 + at, here, :]
            im = links[0, direction * 18 + 9 + at, here, :]
            if ahead:
                acc[row] = acc[row] + re * part[0] - im * part[1]
                acc[3 + row] = acc[3 + row] + re * part[1] + im * part[0]
            else:
                acc[row] = acc[row] + re * part[0] + im * part[1]
                acc[3 + row] = acc[3 + row] + re * part[1] - im * part[0]


def apply_kernel(nz, first, place, *refs):
    links, back, vec, low, high = refs[:5]
    prev = None if first else refs[5]
    out, top, bottom = refs[-3:]
    total = vec.shape[3]
    chunks = total // nz

    def body(n, carry):
        for tile in range(total // TILE):
            here = pl.ds(tile * TILE, TILE)
            acc = [jnp.zeros((TILE, LANES), F32)] * 6
            for direction in range(3):
                hop(links, vec, high, n, total, nz, tile, direction, True, acc)
                hop(back, vec, low, n, total, nz, tile, direction, False, acc)
            for comp in range(6):
                own = vec[0, n, comp, here, :]
                value = ((6.0 * own - acc[comp]) - 7.0 * own) * (1.0 / 5.5)
                if not first:
                    value = 2.0 * value - prev[0, n, comp, here, :]
                out[0, n, comp, here, :] = value
        for comp in range(6):
            top[0, n, comp] = out[0, n, comp, pl.ds(nz - 1, chunks, stride=nz), :]
            bottom[0, n, comp] = out[0, n, comp, pl.ds(0, chunks, stride=nz), :]
        return carry

    lax.fori_loop(0, vec.shape[1], body, 0)


def ahead_kernel(nz, links, vec, high, out):
    total = vec.shape[3]

    def body(n, carry):
        for tile in range(total // TILE):
            acc = [jnp.zeros((TILE, LANES), F32)] * 6
            for direction in range(3):
                hop(links, vec, high, n, total, nz, tile, direction, True, acc)
            for comp in range(6):
                out[0, n, comp, pl.ds(tile * TILE, TILE), :] = acc[comp]
        return carry

    lax.fori_loop(0, vec.shape[1], body, 0)


def gram_kernel(count, *refs):
    left, right, out, total = refs[:count], refs[count:-2], refs[-2], refs[-1]
    tiles = left[0].shape[3] // TILE
    wide = 2 if tiles % 2 == 0 else 1

    def gather(pieces, colour, first):
        rows = []
        for p in range(2):
            for piece in pieces:
                lanes = [
                    piece[0, :, p * 3 + colour, pl.ds((first + j) * TILE, TILE), :].reshape(-1, LANES)
                    for j in range(wide)
                ]
                rows.append(jnp.concatenate(lanes, axis=1) if wide > 1 else lanes[0])
        value = jnp.concatenate(rows, axis=0)
        high = value.astype(jnp.bfloat16)
        return high, (value - high.astype(F32)).astype(jnp.bfloat16)

    def dot(a, b):
        return lax.dot_general(a, b, (((1,), (1,)), ((), ())), preferred_element_type=F32)

    total[...] = jnp.zeros_like(total)
    for colour in range(3):
        for first in range(0, tiles, wide):
            lh, ll = gather(left, colour, first)
            rh, rl = gather(right, colour, first)
            total[...] += dot(lh, rh) + (dot(lh, rl) + dot(ll, rh))

    rows, cols = total.shape
    at_row = lax.broadcasted_iota(jnp.int32, (rows, cols), 0) % TILE
    at_col = lax.broadcasted_iota(jnp.int32, (rows, cols), 1) % TILE
    value = jnp.where(at_row == at_col, total[...], 0.0)

    def picks(n):
        i = lax.broadcasted_iota(jnp.int32, (n // TILE, n), 0)
        j = lax.broadcasted_iota(jnp.int32, (n // TILE, n), 1)
        return jnp.where(j // TILE == i, 1.0, 0.0)

    value = jnp.dot(picks(rows), value, precision=lax.Precision.HIGHEST, preferred_element_type=F32)
    out[0] = lax.dot_general(
        value, picks(cols), (((1,), (1,)), ((), ())),
        precision=lax.Precision.HIGHEST, preferred_element_type=F32,
    )


def sum_kernel(groups, size, mine, out, slots, send_sem, recv_sem):
    count = groups * size
    me = lax.axis_index("cfg") * size + lax.axis_index("sa")

    def device(away):
        other = lax.rem(me + away, count)
        return {"cfg": other // size, "sa": lax.rem(other, size)}

    barrier = pltpu.get_barrier_semaphore()
    for away in range(1, count):
        pl.semaphore_signal(barrier, inc=1, device_id=device(away), device_id_type=pl.DeviceIdType.MESH)
    pl.semaphore_wait(barrier, count - 1)
    copies = []
    for away in range(1, count):
        copy = pltpu.make_async_remote_copy(
            src_ref=mine,
            dst_ref=slots.at[away],
            send_sem=send_sem.at[away],
            recv_sem=recv_sem.at[away],
            device_id=device(away),
            device_id_type=pl.DeviceIdType.MESH,
        )
        copy.start()
        copies.append(copy)
    slots[0] = mine[...]
    for copy in copies:
        copy.wait()
    for group in range(groups):
        value = slots[lax.rem(me + count - group * size, count)]
        for source in range(1, size):
            value = value + slots[lax.rem(me + 2 * count - group * size - source, count)]
        out[group] = value


def sum_blocks(block, groups, size):
    count = groups * size
    return pl.pallas_call(
        functools.partial(sum_kernel, groups, size),
        out_shape=jax.ShapeDtypeStruct((groups,) + block.shape, F32),
        in_specs=[pl.BlockSpec(memory_space=pltpu.VMEM)],
        out_specs=pl.BlockSpec(memory_space=pltpu.VMEM),
        scratch_shapes=[
            pltpu.VMEM((count,) + block.shape, F32),
            pltpu.SemaphoreType.DMA((count,)),
            pltpu.SemaphoreType.DMA((count,)),
        ],
        compiler_params=pltpu.CompilerParams(
            collective_id=0, has_side_effects=True, vmem_limit_bytes=40 * 2**20
        ),
    )(block)


def call(kernel, args, outs, flops=0, place=None, blocks=(), smem=(), scratch=()):
    blocks = dict(blocks)

    def plain(shape):
        return pl.BlockSpec((1,) + tuple(shape[1:]), lambda t, *_: (t,) + (0,) * (len(shape) - 1))

    def spec(at, arg):
        return pl.BlockSpec(*blocks[at]) if at in blocks else plain(arg.shape)

    in_specs = [pl.BlockSpec(memory_space=pltpu.SMEM)] * len(smem) + [spec(i, a) for i, a in enumerate(args)]
    moved = 8 * sum(functools.reduce(lambda x, y: x * y, o) for o in outs)
    scalars = () if place is None else (place,)
    return pl.pallas_call(
        kernel,
        grid_spec=pltpu.PrefetchScalarGridSpec(
            num_scalar_prefetch=len(scalars),
            grid=(outs[0][0],),
            in_specs=in_specs,
            out_specs=[plain(o) for o in outs],
            scratch_shapes=list(scratch),
        ),
        out_shape=[jax.ShapeDtypeStruct(o, F32) for o in outs],
        compiler_params=pltpu.CompilerParams(vmem_limit_bytes=40 * 2**20),
        cost_estimate=pl.CostEstimate(flops=flops, bytes_accessed=moved, transcendentals=0),
    )(*scalars, *smem, *args)


def to_rows(x):
    lead, (nz, sites) = x.shape[:-2], x.shape[-2:]
    x = x.reshape(lead + (nz, sites // LANES, LANES))
    return jnp.swapaxes(x, -3, -2).reshape(lead + (-1, LANES))


def from_rows(x, nz):
    lead, rows = x.shape[:-2], x.shape[-2]
    x = x.reshape(lead + (rows // nz, nz, LANES))
    return jnp.swapaxes(x, -3, -2).reshape(lead + (nz, rows // nz * LANES))


def join_links(links, place, nz):
    rows = to_rows(links.reshape((links.shape[0], 54) + links.shape[5:]))
    half, part = rows.shape[0] // 2, rows.shape[2]
    size = lax.axis_size("sa")
    pairs = [
        (ta * size + sa, (1 - ta) * size + (sa + 1) % size) for ta in range(2) for sa in range(size)
    ]
    start = place[1] * half
    edge = links[:, 2, :, :, :, nz - 1].reshape(2 * half, 18, part // nz, LANES)
    below_mine = from_behind(lax.dynamic_slice_in_dim(edge, start, half, axis=0), "sa", 1)
    below_theirs = lax.ppermute(
        lax.dynamic_slice_in_dim(edge, half - start, half, axis=0), ("ta", "sa"), pairs
    )
    theirs = from_behind(lax.dynamic_slice_in_dim(rows, half - start, half, axis=0), "ta", 1)
    block = ((1,) + rows.shape[1:], lambda t, place: (place[1] * half + t, 0, 0, 0))
    shape = (half, 54, 2 * part, LANES)
    return call(
        functools.partial(join_links_kernel, nz),
        (rows, theirs, below_mine, below_theirs),
        [shape, shape],
        rows.size * 4,
        place=place,
        blocks={0: block},
        scratch=[pltpu.VMEM((1, 18, 2 * part // nz, LANES), F32)],
    )


def on_device(links, vectors):
    nz = vectors.shape[4]
    count_t, count_n = vectors.shape[:2]
    groups = lax.axis_size("cfg")
    me = lax.axis_index("cfg")
    place = jnp.stack([me, lax.axis_index("ta")]).astype(jnp.int32)
    own_n = count_n // groups
    pieces = 2 if own_n % 2 == 0 else 1
    part_n = own_n // pieces

    every = to_rows(vectors.reshape((count_t, count_n, 6) + vectors.shape[4:]))
    total = every.shape[3]
    shape = (count_t, part_n, 6, total, LANES)
    edge = (count_t, part_n, 6, total // nz, LANES)
    own_block = ((1, own_n) + every.shape[2:], lambda t, place: (t, place[0], 0, 0, 0))
    edges = call(
        functools.partial(edges_kernel, nz, pieces), (every,), [edge] * (2 * pieces), place=place, blocks={0: own_block}
    )
    lows = [from_behind(edges[2 * k], "sa", 1) for k in range(pieces)]
    highs = [from_behind(edges[2 * k + 1], "sa", -1) for k in range(pieces)]

    rows, back = join_links(links, place, nz)

    work = count_t * part_n * total * LANES
    fields, older = [every] * pieces, [None] * pieces

    def part(k):
        return ((1, part_n) + every.shape[2:], lambda t, place: (t, place[0] * pieces + k, 0, 0, 0))

    for turn in range(DEG):
        for k in range(pieces):
            args, blocks = (rows, back, fields[k], lows[k], highs[k]), {}
            if turn:
                args = args + (older[k],)
            if turn == 0:
                blocks[2] = part(k)
            if turn == 1:
                blocks[5] = part(k)
            new, top, bottom = call(
                functools.partial(apply_kernel, nz, turn == 0),
                args,
                [shape, edge, edge],
                work * 450,
                place,
                blocks,
            )
            older[k], fields[k] = fields[k], new
            highs[k] = from_behind(bottom, "sa", -1)
            if turn + 1 < DEG:
                lows[k] = from_behind(top, "sa", 1)

    held = [fields] + [[from_behind(f, "cfg", -away) for f in fields] for away in range(1, groups)]
    images = [
        call(functools.partial(ahead_kernel, nz), (rows, fields[k], highs[k]), [shape], work * 220)[0]
        for k in range(pieces)
    ]

    right = fields + images
    side, across = 2 * own_n, 2 * 2 * own_n
    grams = [
        call(
            functools.partial(gram_kernel, pieces),
            held[away] + right,
            [(count_t, side, across)],
            2 * 3 * side * TILE * across * work // part_n,
            scratch=[pltpu.VMEM((side * TILE, across * TILE), F32)],
        )[0]
        for away in range(groups)
    ]
    block = jnp.stack(grams).reshape(-1, LANES)
    raw = sum_blocks(block, groups, lax.axis_size("sa"))
    raw = raw.reshape(groups, groups, count_t, 2, own_n, 2, 2, own_n)
    re = raw[:, :, :, 0, :, 0] + raw[:, :, :, 1, :, 1]
    im = raw[:, :, :, 0, :, 1] - raw[:, :, :, 1, :, 0]
    raw = jnp.moveaxis(jnp.stack([re, im], axis=3), 5, 3)
    raw = jnp.concatenate(
        [
            jnp.concatenate([raw[g, (source - g) % groups] for source in range(groups)], axis=3)
            for g in range(groups)
        ],
        axis=4,
    )
    over, ahead = raw[:, 0], raw[:, 1]
    own_entry = jnp.eye(count_n, dtype=bool)
    inverse = lax.rsqrt(jnp.sum(jnp.where(own_entry, over[:, 0], 0.0), axis=2))
    turned = jnp.swapaxes(ahead, 2, 3)
    lap = 6.0 * over - jnp.stack([ahead[:, 0] + turned[:, 0], ahead[:, 1] - turned[:, 1]], axis=1)
    grams = jnp.stack([over, lap], axis=1)
    grams = grams * inverse[:, None, None, :, None] * inverse[:, None, None, None, :]
    (filtered,) = call(
        functools.partial(scale_kernel, groups, pieces),
        [piece for source in held for piece in source],
        [every.shape],
        place=place,
        smem=(inverse,),
    )
    return (from_rows(filtered, nz).reshape(vectors.shape), grams)


def solution(mesh):
    in_specs = (P(None, None, None, None, None, "sa", "ta"), P("ta", None, None, None, "sa", None))
    out_specs = (
        P(("cfg", "ta"), None, None, None, "sa", None),
        P(("cfg", "ta"), None, None, None, None),
    )
    return jax.shard_map(
        on_device, mesh=mesh, in_specs=in_specs, out_specs=out_specs, check_vma=False
    )
```

```python
import functools

import jax
import jax.numpy as jnp
from jax import lax
from jax.experimental import pallas as pl
from jax.experimental.pallas import tpu as pltpu
from jax.sharding import PartitionSpec as P

LX = 32
DEG = 3
LANES = 128
TILE = 8
F32 = jnp.float32


def from_behind(x, axis, by):
    devices = lax.axis_size(axis)
    return lax.ppermute(x, axis, [(i, (i + by) % devices) for i in range(devices)])


def iota(dim):
    return lax.broadcasted_iota(jnp.int32, (TILE, LANES), dim)


def rows_at(get, total, start):
    if 0 <= start and start + TILE <= total:
        return get(start, TILE)
    base = (start // TILE) * TILE
    offset = start - base
    first, second = get(base % total, TILE), get((base + TILE) % total, TILE)
    return pltpu.roll(jnp.where(iota(0) < offset, second, first), TILE - offset, 0)


def halo_rows(get, nz, tile):
    if nz == 1:
        return get(tile * TILE, TILE)
    out = None
    for part in range(max(TILE // nz, 1)):
        row = jnp.broadcast_to(get((tile * TILE) // nz + part, 1), (TILE, LANES))
        out = row if out is None else jnp.where(iota(0) < part * nz, out, row)
    return out


def shifted(get, halo, total, nz, tile, direction, ahead):
    start, lane = tile * TILE, iota(1)
    if direction == 0:
        here = get(start, TILE)
        if ahead:
            return jnp.where(
                lane % LX == LX - 1, pltpu.roll(here, LX - 1, 1), pltpu.roll(here, LANES - 1, 1)
            )
        return jnp.where(lane % LX == 0, pltpu.roll(here, LANES - LX + 1, 1), pltpu.roll(here, 1, 1))
    if direction == 1:
        here = get(start, TILE)
        if ahead:
            other = rows_at(get, total, start + nz)
            return pltpu.roll(jnp.where(lane < LX, other, here), LANES - LX, 1)
        other = rows_at(get, total, start - nz)
        return pltpu.roll(jnp.where(lane >= LANES - LX, other, here), LX, 1)
    edge = halo_rows(halo, nz, tile)
    if nz == 1:
        return edge
    other = rows_at(get, total, start + (1 if ahead else -1))
    return jnp.where(iota(0) % nz == (nz - 1 if ahead else 0), edge, other)


def reader(ref, *index):
    return lambda start, count: ref[(*index, pl.ds(start, count), slice(None))]


def edges_kernel(nz, pieces, place, vec, *outs):
    own_n, total = vec.shape[1], vec.shape[3]
    chunks, part_n = total // nz, own_n // pieces
    for k in range(pieces):
        top, bottom = outs[2 * k], outs[2 * k + 1]

        def body(n, carry):
            for comp in range(6):
                top[0, n, comp] = vec[0, k * part_n + n, comp, pl.ds(nz - 1, chunks, stride=nz), :]
                bottom[0, n, comp] = vec[0, k * part_n + n, comp, pl.ds(0, chunks, stride=nz), :]
            return carry

        lax.fori_loop(0, part_n, body, 0)


def join_links_kernel(nz, place, mine, theirs, below_mine, below_theirs, out, back, below):
    half, edge = mine.shape[2], below_mine.shape[2]
    total, comps = out.shape[2], out.shape[1] // 3
    ahead = place[1] == 0

    def join(comp, carry):
        a, b = mine[0, comp], theirs[0, comp]
        out[0, comp, pl.ds(0, half), :] = jnp.where(ahead, a, b)
        out[0, comp, pl.ds(half, half), :] = jnp.where(ahead, b, a)
        return carry

    def join_edge(comp, carry):
        a, b = below_mine[0, comp], below_theirs[0, comp]
        below[0, comp, pl.ds(0, edge), :] = jnp.where(ahead, a, b)
        below[0, comp, pl.ds(edge, edge), :] = jnp.where(ahead, b, a)
        return carry

    def body(comp, carry):
        for direction in range(3):
            where = direction * comps + comp
            for tile in range(total // TILE):
                back[0, where, pl.ds(tile * TILE, TILE), :] = shifted(
                    reader(out, 0, where), reader(below, 0, comp), total, nz, tile, direction, False
                )
        return carry

    lax.fori_loop(0, out.shape[1], join, 0)
    lax.fori_loop(0, comps, join_edge, 0)
    lax.fori_loop(0, comps, body, 0)


def scale_kernel(groups, pieces, place, inverse, *refs):
    out = refs[-1]
    t = pl.program_id(0)
    part_n = refs[0].shape[1]
    for away in range(groups):
        source = lax.rem(place[0] + away, groups)
        for k in range(pieces):
            piece = refs[away * pieces + k]
            base = (source * pieces + k) * part_n

            def body(n, carry):
                out[0, base + n] = piece[0, n] * inverse[t, base + n]
                return carry

            lax.fori_loop(0, part_n, body, 0)


def hop(links, vec, halo, n, total, nz, tile, direction, ahead, acc):
    here = pl.ds(tile * TILE, TILE)
    for col in range(3):
        part = [
            shifted(
                reader(vec, 0, n, p * 3 + col),
                None if halo is None else reader(halo, 0, n, p * 3 + col),
                total, nz, tile, direction, ahead,
            )
            for p in range(2)
        ]
        for row in range(3):
            at = (row * 3 + col) if ahead else (col * 3 + row)
            re = links[0, direction * 18 + at, here, :]
            im = links[0, direction * 18 + 9 + at, here, :]
            if ahead:
                acc[row] = acc[row] + re * part[0] - im * part[1]
                acc[3 + row] = acc[3 + row] + re * part[1] + im * part[0]
            else:
                acc[row] = acc[row] + re * part[0] + im * part[1]
                acc[3 + row] = acc[3 + row] + re * part[1] - im * part[0]


def apply_kernel(nz, first, place, *refs):
    links, back, vec, low, high = refs[:5]
    prev = None if first else refs[5]
    out, top, bottom = refs[-3:]
    total = vec.shape[3]
    chunks = total // nz

    def body(n, carry):
        for tile in range(total // TILE):
            here = pl.ds(tile * TILE, TILE)
            acc = [jnp.zeros((TILE, LANES), F32)] * 6
            for direction in range(3):
                hop(links, vec, high, n, total, nz, tile, direction, True, acc)
                hop(back, vec, low, n, total, nz, tile, direction, False, acc)
            for comp in range(6):
                own = vec[0, n, comp, here, :]
                value = ((6.0 * own - acc[comp]) - 7.0 * own) * (1.0 / 5.5)
                if not first:
                    value = 2.0 * value - prev[0, n, comp, here, :]
                out[0, n, comp, here, :] = value
        for comp in range(6):
            top[0, n, comp] = out[0, n, comp, pl.ds(nz - 1, chunks, stride=nz), :]
            bottom[0, n, comp] = out[0, n, comp, pl.ds(0, chunks, stride=nz), :]
        return carry

    lax.fori_loop(0, vec.shape[1], body, 0)


def ahead_kernel(nz, links, vec, high, out):
    total = vec.shape[3]

    def body(n, carry):
        for tile in range(total // TILE):
            acc = [jnp.zeros((TILE, LANES), F32)] * 6
            for direction in range(3):
                hop(links, vec, high, n, total, nz, tile, direction, True, acc)
            for comp in range(6):
                out[0, n, comp, pl.ds(tile * TILE, TILE), :] = acc[comp]
        return carry

    lax.fori_loop(0, vec.shape[1], body, 0)


def gram_kernel(count, *refs):
    left, right, out, total = refs[:count], refs[count:-2], refs[-2], refs[-1]
    tiles = left[0].shape[3] // TILE
    wide = 2 if tiles % 2 == 0 else 1

    def gather(pieces, colour, first):
        rows = []
        for p in range(2):
            for piece in pieces:
                lanes = [
                    piece[0, :, p * 3 + colour, pl.ds((first + j) * TILE, TILE), :].reshape(-1, LANES)
                    for j in range(wide)
                ]
                rows.append(jnp.concatenate(lanes, axis=1) if wide > 1 else lanes[0])
        value = jnp.concatenate(rows, axis=0)
        high = value.astype(jnp.bfloat16)
        return high, (value - high.astype(F32)).astype(jnp.bfloat16)

    def dot(a, b):
        return lax.dot_general(a, b, (((1,), (1,)), ((), ())), preferred_element_type=F32)

    total[...] = jnp.zeros_like(total)
    for colour in range(3):
        for first in range(0, tiles, wide):
            lh, ll = gather(left, colour, first)
            rh, rl = gather(right, colour, first)
            total[...] += dot(lh, rh) + (dot(lh, rl) + dot(ll, rh))

    rows, cols = total.shape
    at_row = lax.broadcasted_iota(jnp.int32, (rows, cols), 0) % TILE
    at_col = lax.broadcasted_iota(jnp.int32, (rows, cols), 1) % TILE
    value = jnp.where(at_row == at_col, total[...], 0.0)

    def picks(n):
        i = lax.broadcasted_iota(jnp.int32, (n // TILE, n), 0)
        j = lax.broadcasted_iota(jnp.int32, (n // TILE, n), 1)
        return jnp.where(j // TILE == i, 1.0, 0.0)

    value = jnp.dot(picks(rows), value, precision=lax.Precision.HIGHEST, preferred_element_type=F32)
    out[0] = lax.dot_general(
        value, picks(cols), (((1,), (1,)), ((), ())),
        precision=lax.Precision.HIGHEST, preferred_element_type=F32,
    )


def sum_kernel(groups, size, mine, out, slots, send_sem, recv_sem):
    count = groups * size
    me = lax.axis_index("cfg") * size + lax.axis_index("sa")

    def device(away):
        other = lax.rem(me + away, count)
        return {"cfg": other // size, "sa": lax.rem(other, size)}

    barrier = pltpu.get_barrier_semaphore()
    for away in range(1, count):
        pl.semaphore_signal(barrier, inc=1, device_id=device(away), device_id_type=pl.DeviceIdType.MESH)
    pl.semaphore_wait(barrier, count - 1)
    copies = []
    for away in range(1, count):
        copy = pltpu.make_async_remote_copy(
            src_ref=mine,
            dst_ref=slots.at[away],
            send_sem=send_sem.at[away],
            recv_sem=recv_sem.at[away],
            device_id=device(away),
            device_id_type=pl.DeviceIdType.MESH,
        )
        copy.start()
        copies.append(copy)
    slots[0] = mine[...]
    for copy in copies:
        copy.wait()
    for group in range(groups):
        value = slots[lax.rem(me + count - group * size, count)]
        for source in range(1, size):
            value = value + slots[lax.rem(me + 2 * count - group * size - source, count)]
        out[group] = value


def sum_blocks(block, groups, size):
    count = groups * size
    return pl.pallas_call(
        functools.partial(sum_kernel, groups, size),
        out_shape=jax.ShapeDtypeStruct((groups,) + block.shape, F32),
        in_specs=[pl.BlockSpec(memory_space=pltpu.VMEM)],
        out_specs=pl.BlockSpec(memory_space=pltpu.VMEM),
        scratch_shapes=[
            pltpu.VMEM((count,) + block.shape, F32),
            pltpu.SemaphoreType.DMA((count,)),
            pltpu.SemaphoreType.DMA((count,)),
        ],
        compiler_params=pltpu.CompilerParams(
            collective_id=0, has_side_effects=True, vmem_limit_bytes=40 * 2**20
        ),
    )(block)


def call(kernel, args, outs, flops=0, place=None, blocks=(), smem=(), scratch=()):
    blocks = dict(blocks)

    def plain(shape):
        return pl.BlockSpec((1,) + tuple(shape[1:]), lambda t, *_: (t,) + (0,) * (len(shape) - 1))

    def spec(at, arg):
        return pl.BlockSpec(*blocks[at]) if at in blocks else plain(arg.shape)

    in_specs = [pl.BlockSpec(memory_space=pltpu.SMEM)] * len(smem) + [spec(i, a) for i, a in enumerate(args)]
    moved = 8 * sum(functools.reduce(lambda x, y: x * y, o) for o in outs)
    scalars = () if place is None else (place,)
    return pl.pallas_call(
        kernel,
        grid_spec=pltpu.PrefetchScalarGridSpec(
            num_scalar_prefetch=len(scalars),
            grid=(outs[0][0],),
            in_specs=in_specs,
            out_specs=[plain(o) for o in outs],
            scratch_shapes=list(scratch),
        ),
        out_shape=[jax.ShapeDtypeStruct(o, F32) for o in outs],
        compiler_params=pltpu.CompilerParams(vmem_limit_bytes=40 * 2**20),
        cost_estimate=pl.CostEstimate(flops=flops, bytes_accessed=moved, transcendentals=0),
    )(*scalars, *smem, *args)


def to_rows(x):
    lead, (nz, sites) = x.shape[:-2], x.shape[-2:]
    x = x.reshape(lead + (nz, sites // LANES, LANES))
    return jnp.swapaxes(x, -3, -2).reshape(lead + (-1, LANES))


def from_rows(x, nz):
    lead, rows = x.shape[:-2], x.shape[-2]
    x = x.reshape(lead + (rows // nz, nz, LANES))
    return jnp.swapaxes(x, -3, -2).reshape(lead + (nz, rows // nz * LANES))


def join_links(links, place, nz):
    rows = to_rows(links.reshape((links.shape[0], 54) + links.shape[5:]))
    half, part = rows.shape[0] // 2, rows.shape[2]
    size = lax.axis_size("sa")
    pairs = [
        (ta * size + sa, (1 - ta) * size + (sa + 1) % size) for ta in range(2) for sa in range(size)
    ]
    start = place[1] * half
    edge = links[:, 2, :, :, :, nz - 1].reshape(2 * half, 18, part // nz, LANES)
    below_mine = from_behind(lax.dynamic_slice_in_dim(edge, start, half, axis=0), "sa", 1)
    below_theirs = lax.ppermute(
        lax.dynamic_slice_in_dim(edge, half - start, half, axis=0), ("ta", "sa"), pairs
    )
    theirs = from_behind(lax.dynamic_slice_in_dim(rows, half - start, half, axis=0), "ta", 1)
    block = ((1,) + rows.shape[1:], lambda t, place: (place[1] * half + t, 0, 0, 0))
    shape = (half, 54, 2 * part, LANES)
    return call(
        functools.partial(join_links_kernel, nz),
        (rows, theirs, below_mine, below_theirs),
        [shape, shape],
        rows.size * 4,
        place=place,
        blocks={0: block},
        scratch=[pltpu.VMEM((1, 18, 2 * part // nz, LANES), F32)],
    )


def on_device(links, vectors):
    nz = vectors.shape[4]
    count_t, count_n = vectors.shape[:2]
    groups = lax.axis_size("cfg")
    me = lax.axis_index("cfg")
    place = jnp.stack([me, lax.axis_index("ta")]).astype(jnp.int32)
    own_n = count_n // groups
    pieces = 2 if own_n % 2 == 0 else 1
    part_n = own_n // pieces

    every = to_rows(vectors.reshape((count_t, count_n, 6) + vectors.shape[4:]))
    total = every.shape[3]
    shape = (count_t, part_n, 6, total, LANES)
    edge = (count_t, part_n, 6, total // nz, LANES)
    own_block = ((1, own_n) + every.shape[2:], lambda t, place: (t, place[0], 0, 0, 0))
    edges = call(
        functools.partial(edges_kernel, nz, pieces), (every,), [edge] * (2 * pieces), place=place, blocks={0: own_block}
    )
    links, edges = lax.optimization_barrier((links, edges))
    lows = [from_behind(edges[2 * k], "sa", 1) for k in range(pieces)]
    highs = [from_behind(edges[2 * k + 1], "sa", -1) for k in range(pieces)]

    rows, back = join_links(links, place, nz)

    work = count_t * part_n * total * LANES
    fields, older = [every] * pieces, [None] * pieces

    def part(k):
        return ((1, part_n) + every.shape[2:], lambda t, place: (t, place[0] * pieces + k, 0, 0, 0))

    for turn in range(DEG):
        for k in range(pieces):
            args, blocks = (rows, back, fields[k], lows[k], highs[k]), {}
            if turn:
                args = args + (older[k],)
            if turn == 0:
                blocks[2] = part(k)
            if turn == 1:
                blocks[5] = part(k)
            new, top, bottom = call(
                functools.partial(apply_kernel, nz, turn == 0),
                args,
                [shape, edge, edge],
                work * 450,
                place,
                blocks,
            )
            older[k], fields[k] = fields[k], new
            highs[k] = from_behind(bottom, "sa", -1)
            if turn + 1 < DEG:
                lows[k] = from_behind(top, "sa", 1)

    held = [fields] + [[from_behind(f, "cfg", -away) for f in fields] for away in range(1, groups)]
    images = [
        call(functools.partial(ahead_kernel, nz), (rows, fields[k], highs[k]), [shape], work * 220)[0]
        for k in range(pieces)
    ]

    right = fields + images
    side, across = 2 * own_n, 2 * 2 * own_n
    grams = [
        call(
            functools.partial(gram_kernel, pieces),
            held[away] + right,
            [(count_t, side, across)],
            2 * 3 * side * TILE * across * work // part_n,
            scratch=[pltpu.VMEM((side * TILE, across * TILE), F32)],
        )[0]
        for away in range(groups)
    ]
    block = jnp.stack(grams).reshape(-1, LANES)
    raw = sum_blocks(block, groups, lax.axis_size("sa"))
    raw = raw.reshape(groups, groups, count_t, 2, own_n, 2, 2, own_n)
    re = raw[:, :, :, 0, :, 0] + raw[:, :, :, 1, :, 1]
    im = raw[:, :, :, 0, :, 1] - raw[:, :, :, 1, :, 0]
    raw = jnp.moveaxis(jnp.stack([re, im], axis=3), 5, 3)
    raw = jnp.concatenate(
        [
            jnp.concatenate([raw[g, (source - g) % groups] for source in range(groups)], axis=3)
            for g in range(groups)
        ],
        axis=4,
    )
    over, ahead = raw[:, 0], raw[:, 1]
    own_entry = jnp.eye(count_n, dtype=bool)
    inverse = lax.rsqrt(jnp.sum(jnp.where(own_entry, over[:, 0], 0.0), axis=2))
    turned = jnp.swapaxes(ahead, 2, 3)
    lap = 6.0 * over - jnp.stack([ahead[:, 0] + turned[:, 0], ahead[:, 1] - turned[:, 1]], axis=1)
    grams = jnp.stack([over, lap], axis=1)
    grams = grams * inverse[:, None, None, :, None] * inverse[:, None, None, None, :]
    (filtered,) = call(
        functools.partial(scale_kernel, groups, pieces),
        [piece for source in held for piece in source],
        [every.shape],
        place=place,
        smem=(inverse,),
    )
    return (from_rows(filtered, nz).reshape(vectors.shape), grams)


def solution(mesh):
    in_specs = (P(None, None, None, None, None, "sa", "ta"), P("ta", None, None, None, "sa", None))
    out_specs = (
        P(("cfg", "ta"), None, None, None, "sa", None),
        P(("cfg", "ta"), None, None, None, None),
    )
    return jax.shard_map(
        on_device, mesh=mesh, in_specs=in_specs, out_specs=out_specs, check_vma=False
    )
```
